32 devices in a mesh: parts: 2 (over y), row: 4 (over z), col: 2 (over x), freq: 2 (over core).
Axes of the slice: x: 2, y: 2, z: 4, core: 2. Of those that a mesh axis runs over, the one named last changes fastest.
Arguments:
- green: float32 [4, 2, 8192, 512], P('freq', None, ('parts', 'row', 'col')), parts along dimension 2, may hold values from -6 to 6
- weights: float32 [8], P(('parts', 'freq')), parts along dimension 0, may hold values from 0.5 to 2
- listed: int32 [64, 9], P(('parts', 'row', 'col')), parts along dimension 0, may hold values 0 or 1
Outputs:
- hessian: float32 [64, 9, 128, 128], P(('parts', 'row', 'col'), None, 'freq'), parts along dimension 0
The draws below stay inside these ranges and needn't reach their ends.
There are 2 independent parts, one for each index of `parts`. The reference program is written for one: setup_inputs(seed, part) draws one part's arguments, and reference() takes and returns one part's arrays. A program takes and returns all parts, laid end to end along the dimension named above; each array names one. Nothing has to cross between parts.
All inputs are finite; a program needn't handle non-finite values. No bound on the sum of `listed` on one device may be relied on, other than what follows from the above.
Results may differ from the reference program's by a relative error of at most 0.00007.
Values sent between devices are 32-bit elements; how exact they have to be, the bound alone decides.
A program may use at most 192 MiB of HBM per device.

```python
import math
import jax
import jax.numpy as jnp
from jax import lax

B = 128
NS = 256
NR = 256
K = 8
K1 = 9
NSR = 512
NB = 32
P_SIZE = 4096
F = 4


def plant(drawn, key, smallest, high):
    place = [jax.random.randint(jax.random.fold_in(key, axis), (), 0, length) for axis, length in enumerate(drawn.shape)]
    main_axis = drawn.shape.index(max(drawn.shape))
    neighbour = place[:main_axis] + [(place[main_axis] + 1) % drawn.shape[main_axis]] + place[main_axis + 1:]
    return drawn.at[tuple(place)].set(smallest).at[tuple(neighbour)].set(high)


def block_scale(stream_key, dims, cuts, least, top_value):
    gain = 1.0
    for axis_at, shards_of in cuts:
        draws = jax.random.uniform(jax.random.fold_in(jax.random.fold_in(stream_key, 6), axis_at), (shards_of,), jnp.float32, least / len(cuts), top_value / len(cuts))
        gain = gain * jnp.repeat(jnp.exp(draws), dims[axis_at] // shards_of).reshape((-1,) + (1,) * (len(dims) - 1 - axis_at))
    return gain


def normal_values(key, extent, width, most, pieces=(), held_as=jnp.bfloat16):
    gain = block_scale(key, extent, pieces, -0.22, 0.18) if pieces else 1.0
    values = jax.random.normal(key, extent, jnp.float32) * width * gain
    return jnp.minimum(jnp.maximum(values, -most), most).astype(held_as)


def setup_inputs(seed: int = 0, part: int = 0) -> dict:
    key_list = jax.random.split(jax.random.key(seed), 4)
    own_keys = jax.random.split(jax.random.fold_in(key_list[3], part), 4)
    green = normal_values(own_keys[0], (F, 2, P_SIZE, NSR), 0.7071, 6.0, ((0, 2), (2, 8)), jnp.float32)
    weights = jnp.clip(jnp.exp(math.log(2.0) - 1.3862944 * jax.random.uniform(own_keys[1], (F,), jnp.float32) ** block_scale(own_keys[1], (F,), ((0, 2),), -0.2, 0.2)), 0.5, 2.0)
    listed = plant((jax.random.randint(own_keys[2], (NB, K1), 0, 4) < 3).astype(jnp.int32), jax.random.fold_in(own_keys[2], 1), 0, 1)
    return dict(green=green, weights=weights, listed=listed)


def half_gram(row_panel, col_panel):
    re_row = row_panel[:, 0]
    im_row = row_panel[:, 1]
    re_col = col_panel[:, 0]
    im_col = col_panel[:, 1]
    left_side = jnp.concatenate([jnp.concatenate([re_row, im_row], -1), jnp.concatenate([im_row, -re_row], -1)], 1)
    right_side = jnp.concatenate([re_col, im_col], -1)
    product = jnp.einsum('fxs,fys->fxy', left_side, right_side, precision=lax.Precision.HIGHEST)
    n = re_row.shape[1]
    return (product[:, :n], product[:, n:])

def gram_tiles(row_panel, col_panel, weights, listed_row):
    source_re, source_im = half_gram(row_panel[..., :NS], col_panel[..., :NS])
    recv_re, recv_im = half_gram(row_panel[..., NS:], col_panel[..., NS:])
    real_part = source_re * recv_re - source_im * recv_im
    weighted = jnp.einsum('f,fxy->xy', weights, real_part, precision=lax.Precision.HIGHEST)
    weighted = weighted * (1.0 / math.sqrt(NS * NR))
    n = weighted.shape[0]
    tile_set = weighted.reshape(n, K1, B).transpose(1, 0, 2)
    return tile_set * listed_row.astype(jnp.float32)[:, None, None]

def reference(green, weights, listed):
    padded = jnp.pad(green, ((0, 0), (0, 0), (0, K * B), (0, 0)))

    def one_block(index):
        start = index * B
        row_panel = lax.dynamic_slice_in_dim(green, start, B, 2)
        col_panel = lax.dynamic_slice_in_dim(padded, start, K1 * B, 2)
        listed_row = lax.dynamic_index_in_dim(listed, index, 0, keepdims=False)
        return gram_tiles(row_panel, col_panel, weights, listed_row)
    return lax.map(one_block, jnp.arange(NB, dtype=jnp.int32))
```

```python
import functools
import math

import jax
import jax.numpy as jnp
from jax import lax
from jax.experimental import pallas as pl
from jax.experimental.pallas import tpu as pltpu
from jax.sharding import PartitionSpec as P

B = 128
Q = 4
K1 = 9
MESH = pl.DeviceIdType.MESH

OWN, OTH, PAR, NB1, NB2 = 0, 4, 8, 12, 16
T_O, T_W, T_A, T_C, T_B, T_END = 0, 10, 26, 36, 52, 62


def stair(r, c):
    return r * (r + 1) // 2 + c


def kernel(rows_n, cols_n, green, weights, listed, out, raw, hi, lo, part, cx, summed, got_m, got_n,
           loc_sem, r_send, r_recv, a_send, a_recv, b_send, b_recv, c_send, c_recv, m_send, m_recv):
    count = rows_n * cols_n
    groups = count // 2
    nsr = green.shape[3]
    ns = nsr // 2
    core = lax.axis_index("freq")
    d = lax.axis_index("row") * cols_n + lax.axis_index("col")
    p = lax.rem(d, 2)
    g = d // 2
    first = p == 0
    up = g < groups - 1
    dn = g > 0
    send1 = jnp.logical_or(jnp.logical_and(first, dn), jnp.logical_and(p == 1, up))
    send2 = jnp.logical_or(jnp.logical_and(first, up), jnp.logical_and(p == 1, dn))

    def at(e):
        e = jnp.clip(e, 0, count - 1)
        return {"row": e // cols_n, "col": lax.rem(e, cols_n)}

    mate = at(d + 1 - 2 * p)
    twin = {"freq": 1 - core}
    to1 = at(d - 2 + 4 * p)
    to2 = at(d + 2 - 4 * p)
    diag = at(d - 1 + 2 * p)

    def remote(src, dst, s, r, dev):
        return pltpu.make_async_remote_copy(
            src_ref=src, dst_ref=dst, send_sem=s, recv_sem=r, device_id=dev, device_id_type=MESH)

    def local(f, j):
        return pltpu.make_async_copy(
            green.at[jnp.where(f == 0, p, 1 - p), :, pl.ds(j * B, B), :], raw.at[f * Q + j], loc_sem.at[f * Q + j])

    def copy_r(j):
        return remote(green.at[1 - p, :, pl.ds(j * B, B), :], raw.at[PAR + j], r_send.at[j], r_recv.at[j], mate)

    def copy_a(j):
        return remote(green.at[p, :, pl.ds(j * B, B), :], raw.at[NB1 + j], a_send.at[j], a_recv.at[j], to1)

    def copy_b(j):
        return remote(raw.at[PAR + j], raw.at[NB2 + j], b_send.at[j], b_recv.at[j], to2)

    for f in range(2):
        for j in range(Q):
            local(f, j).start()

    barrier = pltpu.get_barrier_semaphore()
    pl.semaphore_signal(barrier, inc=1, device_id=twin, device_id_type=MESH)
    pl.semaphore_signal(barrier, inc=1, device_id=mate, device_id_type=MESH)

    @pl.when(send1)
    def _():
        pl.semaphore_signal(barrier, inc=1, device_id=to1, device_id_type=MESH)

    @pl.when(send2)
    def _():
        pl.semaphore_signal(barrier, inc=1, device_id=to2, device_id_type=MESH)

    @pl.when(send1)
    def _():
        pl.semaphore_signal(barrier, inc=1, device_id=diag, device_id_type=MESH)

    pl.semaphore_wait(barrier, 2 + 2 * send1.astype(jnp.int32) + send2.astype(jnp.int32))

    for j in reversed(range(Q)):
        copy_r(j).start()

        @pl.when(send1)
        def _():
            copy_a(j).start()

    def split(slot):
        for part_i in range(2):
            for h in range(2):
                x = raw[slot, part_i, :, h * ns:(h + 1) * ns]
                xh = x.astype(jnp.bfloat16)
                xl = (x - xh.astype(jnp.float32)).astype(jnp.bfloat16)
                base = h * 2 * ns
                a = base + part_i * ns
                b = base + (1 - part_i) * ns
                hi[slot, 0:B, a:a + ns] = xh
                lo[slot, 0:B, a:a + ns] = xl
                hi[slot, B:2 * B, b:b + ns] = -xh if part_i == 1 else xh
                lo[slot, B:2 * B, b:b + ns] = -xl if part_i == 1 else xl

    def gram(rs, cs, h):
        k = slice(h * 2 * ns, (h + 1) * 2 * ns)
        xh, xl, yh, yl = hi[rs, 0:B, k], lo[rs, 0:B, k], hi[cs, :, k], lo[cs, :, k]

        def dot(x, y):
            return lax.dot_general(x, y, (((1,), (1,)), ((), ())), preferred_element_type=jnp.float32)

        return dot(xh, yh) + (dot(xh, yl) + dot(xl, yh))

    def tile(rs, cs):
        s = gram(rs, cs, 0)
        r = gram(rs, cs, 1)
        return s[:, :B] * r[:, :B] - s[:, B:] * r[:, B:]

    scale = 1.0 / math.sqrt(ns * (nsr - ns))
    w_own = weights[p] * scale
    w_oth = weights[1 - p] * scale

    def put(slot, value):
        part[0, slot] = value[:B // 2]
        part[1, slot] = value[B // 2:]

    def cross(start, stop, row_of, col_of, slot_of):
        def body(t, _):
            put(slot_of(t), tile(row_of(t), col_of(t)) * w_own)
            return 0
        lax.fori_loop(start, stop, body, 0)

    def cx_copy(i, a, b):
        return remote(part.at[1 - core, a:b], cx.at[a:b], c_send.at[i], c_recv.at[i], twin)

    def cx_sum(i, a, b):
        cx_copy(i, a, b).wait()

        def body(t, _):
            summed[t] = part[core, t] + cx[t]
            return 0
        lax.fori_loop(a, b, body, 0)

    for f in range(2):
        for j in range(Q):
            local(f, j).wait()

    def split_own(s, _):
        split(s)
        return 0
    lax.fori_loop(0, 2 * Q, split_own, 0)

    for j in range(Q):
        def body(i, _, j=j):
            put(T_O + stair(j, i), tile(OWN + i, OWN + j) * w_own + tile(OTH + i, OTH + j) * w_oth)
            return 0
        lax.fori_loop(0, j + 1, body, 0)
    cx_copy(0, T_O, T_W).start()

    def zero(slot):
        raw[slot] = jnp.zeros(raw.shape[1:], jnp.float32)

    for j in reversed(range(Q)):
        copy_r(j).wait_recv()

        @pl.when(send2)
        def _():
            copy_b(j).start()

        split(PAR + j)
        cross(0, Q,
              lambda t: jnp.where(first, OWN + t, PAR + j),
              lambda t: jnp.where(first, PAR + j, OWN + t),
              lambda t: T_W + jnp.where(first, t * Q + j, j * Q + t))

        @pl.when(send2)
        def _():
            copy_a(j).wait_recv()

        @pl.when(jnp.logical_not(send2))
        def _():
            zero(NB1 + j)

        split(NB1 + j)
        cross(j, Q,
              lambda t: jnp.where(first, OWN, NB1) + t,
              lambda t: jnp.where(first, NB1, OWN) + j,
              lambda t: T_A + stair(t, j))

    cx_copy(1, T_W, T_A).start()
    cx_copy(2, T_A, T_C).start()

    def c_even(t, _):
        put(T_C + t, tile(PAR + t // Q, NB1 + lax.rem(t, Q)) * w_own)
        return 0
    lax.fori_loop(0, jnp.where(first, Q * Q, 0), c_even, 0)

    cx_sum(1, T_W, T_A)
    cx_sum(2, T_A, T_C)

    @pl.when(p == 1)
    def _():
        remote(summed.at[T_W:T_A], got_m, m_send.at[0], m_recv.at[0], mate).start()

    @pl.when(jnp.logical_and(p == 1, dn))
    def _():
        remote(summed.at[T_A:T_C], got_n.at[1], m_send.at[2], m_recv.at[2], to2).start()

    for j in reversed(range(Q)):
        @pl.when(send1)
        def _():
            copy_b(j).wait_recv()

        @pl.when(jnp.logical_not(send1))
        def _():
            zero(NB2 + j)

        split(NB2 + j)
        cross(0, jnp.where(first, 0, Q),
              lambda t: OWN + t,
              lambda t: NB2 + j,
              lambda t: T_C + t * Q + j)
        cross(j, Q,
              lambda t: jnp.where(first, NB2, PAR) + t,
              lambda t: jnp.where(first, PAR, NB2) + j,
              lambda t: T_B + stair(t, j))

    cx_copy(3, T_C, T_B).start()
    cx_copy(4, T_B, T_END).start()

    def flag(r, k):
        return listed[r, k].astype(jnp.float32)

    cx_copy(0, T_O, T_W).wait()
    for j in range(Q):
        for i in range(j + 1):
            s = T_O + stair(j, i)
            out[i, j - i] = (part[core, s] + cx[s]) * flag(i, j - i)

    cx_sum(3, T_C, T_B)

    @pl.when(first)
    def _():
        remote(summed.at[T_C:T_B], got_m, m_send.at[0], m_recv.at[0], mate).start()

    cx_sum(4, T_B, T_END)

    @pl.when(p == 1)
    def _():
        remote(summed.at[T_B:T_END], got_n.at[0], m_send.at[1], m_recv.at[1], mate).start()

    @pl.when(jnp.logical_and(first, dn))
    def _():
        remote(summed.at[T_B:T_END], got_n.at[0], m_send.at[1], m_recv.at[1], diag).start()

    remote(summed.at[T_W:T_A], got_m, m_send.at[0], m_recv.at[0], mate).wait_recv()
    mine = jnp.where(first, T_W, T_C)
    for r in range(Q):
        for c in range(Q):
            out[r, Q + c - r] = (summed[mine + r * Q + c] + got_m[r * Q + c]) * flag(r, Q + c - r)

    n_copy = remote(summed.at[T_B:T_END], got_n.at[0], m_send.at[1], m_recv.at[1], mate)
    n_copy2 = remote(summed.at[T_A:T_C], got_n.at[1], m_send.at[2], m_recv.at[2], to2)

    @pl.when(first)
    def _():
        n_copy.wait_recv()
        for r in range(Q):
            for c in range(r + 1):
                s = stair(r, c)
                out[r, 2 * Q + c - r] = (summed[T_A + s] + got_n[0, s]) * flag(r, 2 * Q + c - r)

    @pl.when(jnp.logical_and(p == 1, up))
    def _():
        n_copy.wait_recv()
        n_copy2.wait_recv()
        for r in range(Q):
            for c in range(r + 1):
                s = stair(r, c)
                out[r, 2 * Q + c - r] = (got_n[0, s] + got_n[1, s]) * flag(r, 2 * Q + c - r)

    @pl.when(jnp.logical_and(p == 1, jnp.logical_not(up)))
    def _():
        for r in range(Q):
            for c in range(r + 1):
                out[r, 2 * Q + c - r] = jnp.zeros((B // 2, B), jnp.float32)

    for j in range(Q):
        copy_r(j).wait_send()

        @pl.when(send1)
        def _():
            copy_a(j).wait_send()

        @pl.when(send2)
        def _():
            copy_b(j).wait_send()

    remote(summed.at[T_W:T_A], got_m, m_send.at[0], m_recv.at[0], mate).wait_send()

    @pl.when(jnp.logical_or(p == 1, dn))
    def _():
        n_copy.wait_send()

    @pl.when(jnp.logical_and(p == 1, dn))
    def _():
        n_copy2.wait_send()


def solution(mesh):
    in_specs = (
        P("freq", None, ("parts", "row", "col"), None),
        P(("parts", "freq")),
        P(("parts", "row", "col"), None),
    )
    out_specs = P(("parts", "row", "col"), None, "freq", None)
    rows_n, cols_n = mesh.shape["row"], mesh.shape["col"]

    def on_device(green, weights, listed):
        nsr = green.shape[3]
        dma = pltpu.SemaphoreType.DMA
        return pl.pallas_call(
            functools.partial(kernel, rows_n, cols_n),
            out_shape=jax.ShapeDtypeStruct((Q, K1, B // 2, B), jnp.float32),
            in_specs=[
                pl.BlockSpec(memory_space=pl.ANY),
                pl.BlockSpec(memory_space=pltpu.SMEM),
                pl.BlockSpec(memory_space=pltpu.SMEM),
            ],
            out_specs=pl.BlockSpec(memory_space=pltpu.VMEM),
            scratch_shapes=[
                pltpu.VMEM((5 * Q, 2, B, nsr), jnp.float32),
                pltpu.VMEM((5 * Q, 2 * B, 2 * nsr), jnp.bfloat16),
                pltpu.VMEM((5 * Q, 2 * B, 2 * nsr), jnp.bfloat16),
                pltpu.VMEM((2, T_END, B // 2, B), jnp.float32),
                pltpu.VMEM((T_END, B // 2, B), jnp.float32),
                pltpu.VMEM((T_END, B // 2, B), jnp.float32),
                pltpu.VMEM((T_A - T_W, B // 2, B), jnp.float32),
                pltpu.VMEM((2, T_C - T_A, B // 2, B), jnp.float32),
                dma((2 * Q,)),
                dma((Q,)), dma((Q,)), dma((Q,)), dma((Q,)), dma((Q,)), dma((Q,)),
                dma((5,)), dma((5,)), dma((3,)), dma((3,)),
            ],
            compiler_params=pltpu.CompilerParams(
                collective_id=0, has_side_effects=True, vmem_limit_bytes=56 * 1024 * 1024),
        )(green, weights, listed)

    return jax.shard_map(on_device, mesh=mesh, in_specs=in_specs, out_specs=out_specs, check_vma=False)
```

```python
import functools
import math

import jax
import jax.numpy as jnp
from jax import lax
from jax.experimental import pallas as pl
from jax.experimental.pallas import tpu as pltpu
from jax.sharding import PartitionSpec as P

B = 128
Q = 4
K1 = 9
MESH = pl.DeviceIdType.MESH

OWN, OTH, PAR, NB1, NB2 = 0, 4, 8, 12, 16
T_O, T_W, T_A, T_C, T_B, T_END = 0, 10, 26, 36, 52, 62


def stair(r, c):
    return r * (r + 1) // 2 + c


def late(r, c):
    return (Q - 1 - c) * (Q - c) // 2 + r - c


def kernel(rows_n, cols_n, green, weights, listed, out, raw, hi, lo, part, cx, summed, got_m, got_n,
           loc_sem, r_send, r_recv, a_send, a_recv, b_send, b_recv, c_send, c_recv, m_send, m_recv):
    count = rows_n * cols_n
    groups = count // 2
    nsr = green.shape[3]
    ns = nsr // 2
    core = lax.axis_index("freq")
    d = lax.axis_index("row") * cols_n + lax.axis_index("col")
    p = lax.rem(d, 2)
    g = d // 2
    first = p == 0
    up = g < groups - 1
    dn = g > 0
    send1 = jnp.logical_or(jnp.logical_and(first, dn), jnp.logical_and(p == 1, up))
    send2 = jnp.logical_or(jnp.logical_and(first, up), jnp.logical_and(p == 1, dn))

    def at(e):
        e = jnp.clip(e, 0, count - 1)
        return {"row": e // cols_n, "col": lax.rem(e, cols_n)}

    mate = at(d + 1 - 2 * p)
    twin = {"freq": 1 - core}
    to1 = at(d - 2 + 4 * p)
    to2 = at(d + 2 - 4 * p)
    diag = at(d - 1 + 2 * p)

    def remote(src, dst, s, r, dev):
        return pltpu.make_async_remote_copy(
            src_ref=src, dst_ref=dst, send_sem=s, recv_sem=r, device_id=dev, device_id_type=MESH)

    def local(f, j):
        return pltpu.make_async_copy(
            green.at[jnp.where(f == 0, p, 1 - p), :, pl.ds(j * B, B), :], raw.at[f * Q + j], loc_sem.at[f * Q + j])

    H = B // 2

    def copy_r(j, h):
        return remote(green.at[1 - p, :, pl.ds(j * B + h * H, H), :], raw.at[PAR + j, :, pl.ds(h * H, H), :],
                      r_send.at[2 * j + h], r_recv.at[2 * j + h], mate)

    def copy_a(j):
        return remote(green.at[p, :, pl.ds(j * B, B), :], raw.at[NB1 + j], a_send.at[j], a_recv.at[j], to1)

    def copy_b(j, h):
        half = pl.ds(h * H, H)
        return remote(raw.at[PAR + j, :, half, :], raw.at[NB2 + j, :, half, :],
                      b_send.at[2 * j + h], b_recv.at[2 * j + h], to2)

    for f in range(2):
        for j in range(Q):
            local(f, j).start()

    barrier = pltpu.get_barrier_semaphore()
    pl.semaphore_signal(barrier, inc=1, device_id=twin, device_id_type=MESH)
    pl.semaphore_signal(barrier, inc=1, device_id=mate, device_id_type=MESH)

    @pl.when(send1)
    def _():
        pl.semaphore_signal(barrier, inc=1, device_id=to1, device_id_type=MESH)

    @pl.when(send2)
    def _():
        pl.semaphore_signal(barrier, inc=1, device_id=to2, device_id_type=MESH)

    @pl.when(send1)
    def _():
        pl.semaphore_signal(barrier, inc=1, device_id=diag, device_id_type=MESH)

    pl.semaphore_wait(barrier, 2 + 2 * send1.astype(jnp.int32) + send2.astype(jnp.int32))

    for j in reversed(range(Q)):
        copy_r(j, 0).start()
        copy_r(j, 1).start()

        @pl.when(send1)
        def _():
            copy_a(j).start()

    def split(slot):
        for part_i in range(2):
            for h in range(2):
                x = raw[slot, part_i, :, h * ns:(h + 1) * ns]
                xh = x.astype(jnp.bfloat16)
                xl = (x - xh.astype(jnp.float32)).astype(jnp.bfloat16)
                base = h * 2 * ns
                a = base + part_i * ns
                b = base + (1 - part_i) * ns
                hi[slot, 0:B, a:a + ns] = xh
                lo[slot, 0:B, a:a + ns] = xl
                hi[slot, B:2 * B, b:b + ns] = -xh if part_i == 1 else xh
                lo[slot, B:2 * B, b:b + ns] = -xl if part_i == 1 else xl

    def gram(rs, cs, h):
        k = slice(h * 2 * ns, (h + 1) * 2 * ns)
        xh, xl, yh, yl = hi[rs, 0:B, k], lo[rs, 0:B, k], hi[cs, :, k], lo[cs, :, k]

        def dot(x, y):
            return lax.dot_general(x, y, (((1,), (1,)), ((), ())), preferred_element_type=jnp.float32)

        return dot(xh, yh) + (dot(xh, yl) + dot(xl, yh))

    def tile(rs, cs):
        s = gram(rs, cs, 0)
        r = gram(rs, cs, 1)
        return s[:, :B] * r[:, :B] - s[:, B:] * r[:, B:]

    scale = 1.0 / math.sqrt(ns * (nsr - ns))
    w_own = weights[p] * scale
    w_oth = weights[1 - p] * scale

    def put(slot, value):
        part[0, slot] = value[:B // 2]
        part[1, slot] = value[B // 2:]

    def cross(start, stop, row_of, col_of, slot_of):
        def body(t, _):
            put(slot_of(t), tile(row_of(t), col_of(t)) * w_own)
            return 0
        lax.fori_loop(start, stop, body, 0)

    def cx_copy(i, a, n):
        return remote(part.at[1 - core, pl.ds(a, n)], cx.at[pl.ds(a, n)], c_send.at[i], c_recv.at[i], twin)

    def cx_sum(i, a, n):
        cx_copy(i, a, n).wait()

        def body(t, _):
            summed[a + t] = part[core, a + t] + cx[a + t]
            return 0
        lax.fori_loop(0, n, body, 0)

    for f in range(2):
        for j in range(Q):
            local(f, j).wait()

    def split_own(s, _):
        split(s)
        return 0
    lax.fori_loop(0, 2 * Q, split_own, 0)

    for j in range(Q):
        def body(i, _, j=j):
            put(T_O + stair(j, i), tile(OWN + i, OWN + j) * w_own + tile(OTH + i, OTH + j) * w_oth)
            return 0
        lax.fori_loop(0, j + 1, body, 0)
    cx_copy(0, T_O, T_W - T_O).start()

    def zero(slot):
        raw[slot] = jnp.zeros(raw.shape[1:], jnp.float32)

    n_full, n_tri = Q * Q, T_C - T_A
    away = jnp.where(first, T_C, T_W)
    kept = jnp.where(first, T_W, T_C)

    def send_m():
        return remote(summed.at[pl.ds(away, n_full)], got_m, m_send.at[0], m_recv.at[0], mate)

    def send_n(i, dev):
        a, n = ((0, n_tri - Q), (n_tri - Q, Q))[i]
        return remote(summed.at[pl.ds(T_B + a, n)], got_n.at[0, pl.ds(a, n)], m_send.at[1 + i], m_recv.at[1 + i], dev)

    def send_a():
        return remote(summed.at[pl.ds(T_A, n_tri)], got_n.at[1], m_send.at[3], m_recv.at[3], to2)

    def start_n(i):
        @pl.when(p == 1)
        def _():
            send_n(i, mate).start()

        @pl.when(jnp.logical_and(first, dn))
        def _():
            send_n(i, diag).start()

    def flag(r, k):
        return listed[r, k].astype(jnp.float32)

    for j in reversed(range(Q)):
        for h in range(2):
            copy_r(j, h).wait_recv()

            @pl.when(send2)
            def _():
                copy_b(j, h).start()

        split(PAR + j)

        @pl.when(send2)
        def _():
            copy_a(j).wait_recv()

        @pl.when(jnp.logical_not(send2))
        def _():
            zero(NB1 + j)

        split(NB1 + j)

        def cr(t):
            return jnp.where(t < Q - j, j, t - (Q - j) + j + 1)

        def cc(t):
            return jnp.where(t < Q - j, j + t, j)

        cross(0, jnp.where(first, 2 * (Q - j) - 1, Q),
              lambda t: jnp.where(first, PAR + cr(t), PAR + j),
              lambda t: jnp.where(first, NB1 + cc(t), OWN + t),
              lambda t: jnp.where(first, T_C + cr(t) * Q + cc(t), T_W + j * Q + t))
        if j == 0:
            cx_copy(1, away, n_full).start()
        cross(j, Q,
              lambda t: jnp.where(first, OWN, NB1) + t,
              lambda t: jnp.where(first, NB1, OWN) + j,
              lambda t: T_A + late(t, j))
        if j == 0:
            cx_copy(2, T_A, n_tri).start()
            cx_sum(1, away, n_full)
            send_m().start()
        cross(0, jnp.where(first, Q, 0),
              lambda t: OWN + t,
              lambda t: PAR + j,
              lambda t: T_W + t * Q + j)

    cx_sum(2, T_A, n_tri)

    @pl.when(jnp.logical_and(p == 1, dn))
    def _():
        send_a().start()

    for j in reversed(range(Q)):
        if j == 0:
            cx_copy(0, T_O, T_W - T_O).wait()
            for b in range(Q):
                for a in range(b + 1):
                    s = T_O + stair(b, a)
                    out[a, b - a] = (part[core, s] + cx[s]) * flag(a, b - a)

        @pl.when(send1)
        def _():
            copy_b(j, 0).wait_recv()
            copy_b(j, 1).wait_recv()

        @pl.when(jnp.logical_not(send1))
        def _():
            zero(NB2 + j)

        split(NB2 + j)
        cross(j, Q,
              lambda t: jnp.where(first, NB2, PAR) + t,
              lambda t: jnp.where(first, PAR, NB2) + j,
              lambda t: T_B + late(t, j))
        if j == 1:
            cx_copy(4, T_B, n_tri - Q).start()
        if j == 0:
            cx_copy(5, T_B + n_tri - Q, Q).start()
        cross(0, jnp.where(first, 0, Q),
              lambda t: OWN + t,
              lambda t: NB2 + j,
              lambda t: T_C + t * Q + j)
        if j == 1:
            cx_sum(4, T_B, n_tri - Q)
            start_n(0)

    cx_copy(3, kept, n_full).start()
    cx_sum(5, T_B + n_tri - Q, Q)
    start_n(1)
    cx_sum(3, kept, n_full)

    send_m().wait_recv()
    for r in range(Q):
        for c in range(Q):
            out[r, Q + c - r] = (summed[kept + r * Q + c] + got_m[r * Q + c]) * flag(r, Q + c - r)

    @pl.when(first)
    def _():
        send_n(0, mate).wait_recv()
        send_n(1, mate).wait_recv()
        for r in range(Q):
            for c in range(r + 1):
                s = late(r, c)
                out[r, 2 * Q + c - r] = (summed[T_A + s] + got_n[0, s]) * flag(r, 2 * Q + c - r)

    @pl.when(jnp.logical_and(p == 1, up))
    def _():
        send_a().wait_recv()
        send_n(0, mate).wait_recv()
        send_n(1, mate).wait_recv()
        for r in range(Q):
            for c in range(r + 1):
                s = late(r, c)
                out[r, 2 * Q + c - r] = (got_n[0, s] + got_n[1, s]) * flag(r, 2 * Q + c - r)

    @pl.when(jnp.logical_and(p == 1, jnp.logical_not(up)))
    def _():
        for r in range(Q):
            for c in range(r + 1):
                out[r, 2 * Q + c - r] = jnp.zeros((B // 2, B), jnp.float32)

    for j in range(Q):
        for h in range(2):
            copy_r(j, h).wait_send()

            @pl.when(send2)
            def _():
                copy_b(j, h).wait_send()

        @pl.when(send1)
        def _():
            copy_a(j).wait_send()

    send_m().wait_send()

    @pl.when(jnp.logical_or(p == 1, dn))
    def _():
        send_n(0, mate).wait_send()
        send_n(1, mate).wait_send()

    @pl.when(jnp.logical_and(p == 1, dn))
    def _():
        send_a().wait_send()


def solution(mesh):
    in_specs = (
        P("freq", None, ("parts", "row", "col"), None),
        P(("parts", "freq")),
        P(("parts", "row", "col"), None),
    )
    out_specs = P(("parts", "row", "col"), None, "freq", None)
    rows_n, cols_n = mesh.shape["row"], mesh.shape["col"]

    def on_device(green, weights, listed):
        nsr = green.shape[3]
        dma = pltpu.SemaphoreType.DMA
        return pl.pallas_call(
            functools.partial(kernel, rows_n, cols_n),
            out_shape=jax.ShapeDtypeStruct((Q, K1, B // 2, B), jnp.float32),
            in_specs=[
                pl.BlockSpec(memory_space=pl.ANY),
                pl.BlockSpec(memory_space=pltpu.SMEM),
                pl.BlockSpec(memory_space=pltpu.SMEM),
            ],
            out_specs=pl.BlockSpec(memory_space=pltpu.VMEM),
            scratch_shapes=[
                pltpu.VMEM((5 * Q, 2, B, nsr), jnp.float32),
                pltpu.VMEM((5 * Q, 2 * B, 2 * nsr), jnp.bfloat16),
                pltpu.VMEM((5 * Q, 2 * B, 2 * nsr), jnp.bfloat16),
                pltpu.VMEM((2, T_END, B // 2, B), jnp.float32),
                pltpu.VMEM((T_END, B // 2, B), jnp.float32),
                pltpu.VMEM((T_END, B // 2, B), jnp.float32),
                pltpu.VMEM((T_A - T_W, B // 2, B), jnp.float32),
                pltpu.VMEM((2, T_C - T_A, B // 2, B), jnp.float32),
                dma((2 * Q,)),
                dma((2 * Q,)), dma((2 * Q,)), dma((Q,)), dma((Q,)), dma((2 * Q,)), dma((2 * Q,)),
                dma((6,)), dma((6,)), dma((4,)), dma((4,)),
            ],
            compiler_params=pltpu.CompilerParams(
                collective_id=0, has_side_effects=True, vmem_limit_bytes=56 * 1024 * 1024),
        )(green, weights, listed)

    return jax.shard_map(on_device, mesh=mesh, in_specs=in_specs, out_specs=out_specs, check_vma=False)
```

```python
import functools
import math

import jax
import jax.numpy as jnp
from jax import lax
from jax.experimental import pallas as pl
from jax.experimental.pallas import tpu as pltpu
from jax.sharding import PartitionSpec as P

B = 128
Q = 4
K1 = 9
MESH = pl.DeviceIdType.MESH

OWN, OTH, PAR, NB1, NB2 = 0, 4, 8, 12, 16
T_O, T_W, T_A, T_C, T_B, T_END = 0, 10, 26, 36, 52, 62
GROUP = 2


def stair(r, c):
    return r * (r + 1) // 2 + c


def late(r, c):
    return (Q - 1 - c) * (Q - c) // 2 + r - c


def kernel(rows_n, cols_n, green, weights, listed, out, raw, hi, lo, part, cx, summed, got_m, got_n,
           loc_sem, r_send, r_recv, a_send, a_recv, b_send, b_recv, c_send, c_recv, m_send, m_recv):
    count = rows_n * cols_n
    groups = count // 2
    nsr = green.shape[3]
    ns = nsr // 2
    core = lax.axis_index("freq")
    d = lax.axis_index("row") * cols_n + lax.axis_index("col")
    p = lax.rem(d, 2)
    g = d // 2
    first = p == 0
    up = g < groups - 1
    dn = g > 0
    send1 = jnp.logical_or(jnp.logical_and(first, dn), jnp.logical_and(p == 1, up))
    send2 = jnp.logical_or(jnp.logical_and(first, up), jnp.logical_and(p == 1, dn))

    def at(e):
        e = jnp.clip(e, 0, count - 1)
        return {"row": e // cols_n, "col": lax.rem(e, cols_n)}

    mate = at(d + 1 - 2 * p)
    twin = {"freq": 1 - core}
    to1 = at(d - 2 + 4 * p)
    to2 = at(d + 2 - 4 * p)
    diag = at(d - 1 + 2 * p)

    def remote(src, dst, s, r, dev):
        return pltpu.make_async_remote_copy(
            src_ref=src, dst_ref=dst, send_sem=s, recv_sem=r, device_id=dev, device_id_type=MESH)

    def local(f, j):
        return pltpu.make_async_copy(
            green.at[jnp.where(f == 0, p, 1 - p), :, pl.ds(j * B, B), :], raw.at[f * Q + j], loc_sem.at[f * Q + j])

    H = B // 2

    def copy_r(j, h):
        return remote(green.at[1 - p, :, pl.ds(j * B + h * H, H), :], raw.at[PAR + j, :, pl.ds(h * H, H), :],
                      r_send.at[2 * j + h], r_recv.at[2 * j + h], mate)

    def copy_a(j):
        return remote(green.at[p, :, pl.ds(j * B, B), :], raw.at[NB1 + j], a_send.at[j], a_recv.at[j], to1)

    def copy_b(j, h):
        half = pl.ds(h * H, H)
        return remote(raw.at[PAR + j, :, half, :], raw.at[NB2 + j, :, half, :],
                      b_send.at[2 * j + h], b_recv.at[2 * j + h], to2)

    for f in range(2):
        for j in range(Q):
            local(f, j).start()

    barrier = pltpu.get_barrier_semaphore()
    pl.semaphore_signal(barrier, inc=1, device_id=twin, device_id_type=MESH)
    pl.semaphore_signal(barrier, inc=1, device_id=mate, device_id_type=MESH)

    @pl.when(send1)
    def _():
        pl.semaphore_signal(barrier, inc=1, device_id=to1, device_id_type=MESH)

    @pl.when(send2)
    def _():
        pl.semaphore_signal(barrier, inc=1, device_id=to2, device_id_type=MESH)

    @pl.when(send1)
    def _():
        pl.semaphore_signal(barrier, inc=1, device_id=diag, device_id_type=MESH)

    pl.semaphore_wait(barrier, 2 + 2 * send1.astype(jnp.int32) + send2.astype(jnp.int32))

    for j in reversed(range(Q)):
        copy_r(j, 0).start()
        copy_r(j, 1).start()

        @pl.when(send1)
        def _():
            copy_a(j).start()

    def split(slot):
        for part_i in range(2):
            for h in range(2):
                x = raw[slot, part_i, :, h * ns:(h + 1) * ns]
                xh = x.astype(jnp.bfloat16)
                xl = (x - xh.astype(jnp.float32)).astype(jnp.bfloat16)
                base = h * 2 * ns
                a = base + part_i * ns
                b = base + (1 - part_i) * ns
                hi[slot, 0:B, a:a + ns] = xh
                lo[slot, 0:B, a:a + ns] = xl
                hi[slot, B:2 * B, b:b + ns] = -xh if part_i == 1 else xh
                lo[slot, B:2 * B, b:b + ns] = -xl if part_i == 1 else xl

    def gram(rs, n, cs, h):
        k = slice(h * 2 * ns, (h + 1) * 2 * ns)
        xh = hi[pl.ds(rs, n), 0:B, k].reshape(n * B, 2 * ns)
        xl = lo[pl.ds(rs, n), 0:B, k].reshape(n * B, 2 * ns)

        def dot(x, y):
            return lax.dot_general(x, y, (((1,), (1,)), ((), ())), preferred_element_type=jnp.float32)

        both = dot(jnp.concatenate([xh, xl], 0), hi[cs, :, k])
        return both[:n * B] + (both[n * B:] + dot(xh, lo[cs, :, k]))

    def tiles(rs, n, cs):
        s = gram(rs, n, cs, 0)
        r = gram(rs, n, cs, 1)
        return s[:, :B] * r[:, :B] - s[:, B:] * r[:, B:]

    scale = 1.0 / math.sqrt(ns * (nsr - ns))
    w_own = weights[p] * scale
    w_oth = weights[1 - p] * scale

    def put(slot, value):
        part[0, slot] = value[:B // 2]
        part[1, slot] = value[B // 2:]

    def runs(start, stop):
        return [(t, min(GROUP, stop - t)) for t in range(start, stop, GROUP)]

    def cross(start, stop, row, col, slot_of, flip=False):
        for t, n in runs(start, stop):
            value = tiles(row + t, n, col) * w_own
            for i in range(n):
                one = value[i * B:(i + 1) * B]
                put(slot_of(t + i), one.T if flip else one)

    def cx_copy(i, a, n):
        return remote(part.at[1 - core, pl.ds(a, n)], cx.at[pl.ds(a, n)], c_send.at[i], c_recv.at[i], twin)

    def cx_sum(i, a, n):
        cx_copy(i, a, n).wait()

        def body(t, _):
            summed[a + t] = part[core, a + t] + cx[a + t]
            return 0
        lax.fori_loop(0, n, body, 0)

    for f in range(2):
        for j in range(Q):
            local(f, j).wait()

    def split_own(s, _):
        split(s)
        return 0
    lax.fori_loop(0, 2 * Q, split_own, 0)

    for j in range(Q):
        for t, n in runs(0, j + 1):
            value = tiles(OWN + t, n, OWN + j) * w_own + tiles(OTH + t, n, OTH + j) * w_oth
            for i in range(n):
                put(T_O + stair(j, t + i), value[i * B:(i + 1) * B])
    cx_copy(0, T_O, T_W - T_O).start()

    def zero(slot):
        raw[slot] = jnp.zeros(raw.shape[1:], jnp.float32)

    n_full, n_tri = Q * Q, T_C - T_A
    away = jnp.where(first, T_C, T_W)
    kept = jnp.where(first, T_W, T_C)

    def send_m():
        return remote(summed.at[pl.ds(away, n_full)], got_m, m_send.at[0], m_recv.at[0], mate)

    def send_n(i, dev):
        a, n = ((0, n_tri - Q), (n_tri - Q, Q))[i]
        return remote(summed.at[pl.ds(T_B + a, n)], got_n.at[0, pl.ds(a, n)], m_send.at[1 + i], m_recv.at[1 + i], dev)

    def send_a():
        return remote(summed.at[pl.ds(T_A, n_tri)], got_n.at[1], m_send.at[3], m_recv.at[3], to2)

    def start_n(i):
        @pl.when(p == 1)
        def _():
            send_n(i, mate).start()

        @pl.when(jnp.logical_and(first, dn))
        def _():
            send_n(i, diag).start()

    def flag(r, k):
        return listed[r, k].astype(jnp.float32)

    for j in reversed(range(Q)):
        for h in range(2):
            copy_r(j, h).wait_recv()

            @pl.when(send2)
            def _():
                copy_b(j, h).start()

        split(PAR + j)

        @pl.when(send2)
        def _():
            copy_a(j).wait_recv()

        @pl.when(jnp.logical_not(send2))
        def _():
            zero(NB1 + j)

        split(NB1 + j)

        @pl.when(first)
        def _():
            cross(j, Q, PAR, NB1 + j, lambda t: T_C + t * Q + j)
            cross(j + 1, Q, NB1, PAR + j, lambda t: T_C + j * Q + t, flip=True)

        @pl.when(p == 1)
        def _():
            cross(0, Q, OWN, PAR + j, lambda t: T_W + j * Q + t, flip=True)

        if j == 0:
            cx_copy(1, away, n_full).start()
        cross(j, Q, jnp.where(first, OWN, NB1), jnp.where(first, NB1, OWN) + j, lambda t: T_A + late(t, j))
        if j == 0:
            cx_copy(2, T_A, n_tri).start()
            cx_sum(1, away, n_full)
            send_m().start()

        @pl.when(first)
        def _():
            cross(0, Q, OWN, PAR + j, lambda t: T_W + t * Q + j)

    cx_sum(2, T_A, n_tri)

    @pl.when(jnp.logical_and(p == 1, dn))
    def _():
        send_a().start()

    for j in reversed(range(Q)):
        if j == 0:
            cx_copy(0, T_O, T_W - T_O).wait()
            for b in range(Q):
                for a in range(b + 1):
                    s = T_O + stair(b, a)
                    out[a, b - a] = (part[core, s] + cx[s]) * flag(a, b - a)

        @pl.when(send1)
        def _():
            copy_b(j, 0).wait_recv()
            copy_b(j, 1).wait_recv()

        @pl.when(jnp.logical_not(send1))
        def _():
            zero(NB2 + j)

        split(NB2 + j)
        cross(j, Q, jnp.where(first, NB2, PAR), jnp.where(first, PAR, NB2) + j, lambda t: T_B + late(t, j))
        if j == 1:
            cx_copy(4, T_B, n_tri - Q).start()
        if j == 0:
            cx_copy(5, T_B + n_tri - Q, Q).start()

        @pl.when(p == 1)
        def _():
            cross(0, Q, OWN, NB2 + j, lambda t: T_C + t * Q + j)

        if j == 1:
            cx_sum(4, T_B, n_tri - Q)
            start_n(0)

    cx_copy(3, kept, n_full).start()
    cx_sum(5, T_B + n_tri - Q, Q)
    start_n(1)
    cx_sum(3, kept, n_full)

    send_m().wait_recv()
    for r in range(Q):
        for c in range(Q):
            out[r, Q + c - r] = (summed[kept + r * Q + c] + got_m[r * Q + c]) * flag(r, Q + c - r)

    @pl.when(first)
    def _():
        send_n(0, mate).wait_recv()
        send_n(1, mate).wait_recv()
        for r in range(Q):
            for c in range(r + 1):
                s = late(r, c)
                out[r, 2 * Q + c - r] = (summed[T_A + s] + got_n[0, s]) * flag(r, 2 * Q + c - r)

    @pl.when(jnp.logical_and(p == 1, up))
    def _():
        send_a().wait_recv()
        send_n(0, mate).wait_recv()
        send_n(1, mate).wait_recv()
        for r in range(Q):
            for c in range(r + 1):
                s = late(r, c)
                out[r, 2 * Q + c - r] = (got_n[0, s] + got_n[1, s]) * flag(r, 2 * Q + c - r)

    @pl.when(jnp.logical_and(p == 1, jnp.logical_not(up)))
    def _():
        for r in range(Q):
            for c in range(r + 1):
                out[r, 2 * Q + c - r] = jnp.zeros((B // 2, B), jnp.float32)

    for j in range(Q):
        for h in range(2):
            copy_r(j, h).wait_send()

            @pl.when(send2)
            def _():
                copy_b(j, h).wait_send()

        @pl.when(send1)
        def _():
            copy_a(j).wait_send()

    send_m().wait_send()

    @pl.when(jnp.logical_or(p == 1, dn))
    def _():
        send_n(0, mate).wait_send()
        send_n(1, mate).wait_send()

    @pl.when(jnp.logical_and(p == 1, dn))
    def _():
        send_a().wait_send()


def solution(mesh):
    in_specs = (
        P("freq", None, ("parts", "row", "col"), None),
        P(("parts", "freq")),
        P(("parts", "row", "col"), None),
    )
    out_specs = P(("parts", "row", "col"), None, "freq", None)
    rows_n, cols_n = mesh.shape["row"], mesh.shape["col"]

    def on_device(green, weights, listed):
        nsr = green.shape[3]
        dma = pltpu.SemaphoreType.DMA
        return pl.pallas_call(
            functools.partial(kernel, rows_n, cols_n),
            out_shape=jax.ShapeDtypeStruct((Q, K1, B // 2, B), jnp.float32),
            in_specs=[
                pl.BlockSpec(memory_space=pl.ANY),
                pl.BlockSpec(memory_space=pltpu.SMEM),
                pl.BlockSpec(memory_space=pltpu.SMEM),
            ],
            out_specs=pl.BlockSpec(memory_space=pltpu.VMEM),
            scratch_shapes=[
                pltpu.VMEM((5 * Q, 2, B, nsr), jnp.float32),
                pltpu.VMEM((5 * Q, 2 * B, 2 * nsr), jnp.bfloat16),
                pltpu.VMEM((5 * Q, 2 * B, 2 * nsr), jnp.bfloat16),
                pltpu.VMEM((2, T_END, B // 2, B), jnp.float32),
                pltpu.VMEM((T_END, B // 2, B), jnp.float32),
                pltpu.VMEM((T_END, B // 2, B), jnp.float32),
                pltpu.VMEM((T_A - T_W, B // 2, B), jnp.float32),
                pltpu.VMEM((2, T_C - T_A, B // 2, B), jnp.float32),
                dma((2 * Q,)),
                dma((2 * Q,)), dma((2 * Q,)), dma((Q,)), dma((Q,)), dma((2 * Q,)), dma((2 * Q,)),
                dma((6,)), dma((6,)), dma((4,)), dma((4,)),
            ],
            compiler_params=pltpu.CompilerParams(
                collective_id=0, has_side_effects=True, vmem_limit_bytes=56 * 1024 * 1024),
        )(green, weights, listed)

    return jax.shard_map(on_device, mesh=mesh, in_specs=in_specs, out_specs=out_specs, check_vma=False)
```
